32 devices in a mesh: groups: 2 (over x), ctx: 16 (over z, y, core).
Axes of the slice: x: 2, y: 2, z: 4, core: 2. Of those that a mesh axis runs over, the one named last changes fastest.
Arguments:
- patches: bfloat16 [128, 3200], P(('groups', 'ctx')), parts along dimension 0, may hold values from -60 to 60
- vit_gain: float32 [3200], replicated, may hold values from 0.1 to 1.9
- vit_fc1: bfloat16 [3200, 12800], P(None, 'ctx'), may hold values from -0.109375 to 0.109375
- vit_fc2: bfloat16 [12800, 3200], P('ctx'), may hold values from -0.0546875 to 0.0546875
- proj_gain: float32 [12800], replicated, may hold values from 0.1 to 1.9
- proj_bias: float32 [12800], replicated, may hold values from -3 to 3
- proj_weight: bfloat16 [12800, 8192], P(None, 'ctx'), may hold values from -0.0546875 to 0.0546875
- llm_gain: float32 [8192], P('ctx'), may hold values from 0.1 to 1.9
- qkv_weight: bfloat16 [8192, 10240], P('ctx'), may hold values from -0.0625 to 0.0625
- text_query: bfloat16 [2048, 8192], P(('groups', 'ctx')), parts along dimension 0, may hold values from -130 to 130
- text_keyvalue: bfloat16 [2048, 2048], P(('groups', 'ctx')), parts along dimension 0, may hold values from -6 to 6
- doc_ids: int32 [2048], P(('groups', 'ctx')), parts along dimension 0, may hold values from 0 to 3, never falling along the last dimension, each value on 1 to 640 neighbouring positions
- image_positions: int32 [32], P('groups'), parts along dimension 0, may hold values from 0 to 1023, as said below
Outputs:
- attended: bfloat16 [2048, 8192], P(('groups', 'ctx')), parts along dimension 0
The draws below stay inside these ranges and needn't reach their ends.
There are 2 independent parts, one for each index of `groups`. The reference program is written for one: setup_inputs(seed, part) draws one part's arguments, and reference() takes and returns one part's arrays. A program takes and returns all parts, laid end to end along the dimension named above; an argument that names none is the same for every part. Nothing has to cross between parts.
Inputs may be any that keep to these rules, and one draw needn't show every extreme that they name: `image_positions`: strictly increasing; of the 64 positions of one shard (starting at a multiple of 64) at most 2 hold image tokens, and some shard holds exactly 2.
All inputs are finite; a program needn't handle non-finite values.
Results may differ from the reference program's by a relative error of at most 0.0044.
Values may be sent and summed in bfloat16 or wider, within the bound.
A program may use at most 192 MiB of HBM per device.

```python
import math
import jax
import jax.numpy as jnp
import numpy as np
from jax import lax

DV = 3200
FFV = 12800
SHUF = 4
D = 8192
QH = 64
KVH = 8
HD = 128
QKVW = 10240
S_DEV = 64
PATCHES = 64
IMG = 16
CAP = 2
SEQ = 1024
N_CTX = 16


def shared_keys(key):
    return jax.random.truncated_normal(key, -6.0, 6.0, (SEQ, KVH, HD), jnp.float32)


def draw_text_keyvalue(key, part):
    key_rows = shared_keys(key)
    key = jax.random.fold_in(key, 5)
    value_rows = jax.random.truncated_normal(key, -6.0, 6.0, (SEQ, KVH, HD), jnp.float32)
    return jnp.concatenate([key_rows.reshape(SEQ, KVH * HD), value_rows.reshape(SEQ, KVH * HD)], axis=1).astype(jnp.bfloat16)


def draw_text_query(key, part):
    key = jax.random.fold_in(key, 4)
    query_rows = jax.random.truncated_normal(key, -6.0, 6.0, (SEQ, QH, HD), jnp.float32)
    return query_rows.reshape(SEQ, QH * HD).astype(jnp.bfloat16)


def draw_patches(key, part):
    key = jax.random.fold_in(key, 9)
    base_key, column_key, row_key = jax.random.split(key, 3)
    column_pos = jnp.arange(DV, dtype=jnp.float32)
    column_scale = 10.0 ** (jax.random.uniform(column_key, (DV,), jnp.float32) - 0.5) * 3.0 ** (column_pos / DV - 0.5)
    row_scale = 10.0 ** (0.5 * jax.random.uniform(row_key, (PATCHES, 1), jnp.float32) - 0.25)
    noise = jax.random.truncated_normal(base_key, -6.0, 6.0, (PATCHES, DV), jnp.float32)
    return (noise * column_scale[None, :] * row_scale).astype(jnp.bfloat16)


def draw_image_positions(key, part):
    key = jax.random.fold_in(key, 11)
    order_key, full_key, row_key = jax.random.split(key, 3)
    slot_total = N_CTX * CAP
    slot_ids = jnp.arange(slot_total, dtype=jnp.int32)
    priority = jax.random.permutation(order_key, slot_total).astype(jnp.int32)
    full_shard = jax.random.randint(full_key, (), 0, N_CTX, dtype=jnp.int32)
    priority = jnp.where(slot_ids // CAP == full_shard, slot_ids % CAP - CAP, priority)
    chosen = jnp.sort(jnp.argsort(priority, stable=True)[:IMG]).astype(jnp.int32)
    rows_table = jnp.tile(jnp.arange(S_DEV, dtype=jnp.int32)[None, :], (N_CTX, 1))
    rows_table = jax.random.permutation(row_key, rows_table, axis=1, independent=True)
    rows_table = jnp.sort(rows_table[:, :CAP], axis=1)
    owner_shard = chosen // CAP
    return (owner_shard * S_DEV + rows_table[owner_shard, chosen % CAP]).astype(jnp.int32)


def level_of(own_key, shape, cuts, least, largest):
    def one(position, parts):
        heights = jax.random.uniform(jax.random.fold_in(jax.random.fold_in(own_key, 6), position), (parts,), jnp.float32, least / len(cuts), largest / len(cuts))
        return jnp.repeat(jnp.exp(heights), shape[position] // parts).reshape((-1,) + (1,) * (len(shape) - position - 1))

    loudness = one(*cuts[0])
    for cut in cuts[1:]:
        loudness = loudness * one(*cut)
    return loudness


def split_up(number_of, total, most, lean):
    portions = [(1 << 20) // math.isqrt(standing ** lean) + 1 for standing in range(2, number_of + 1)]
    rest, holding = total - most - (number_of - 1), [1] * (number_of - 1)
    while rest > 0:
        candidates = [i for i in range(number_of - 1) if holding[i] < most]
        whole, remaining = sum([portions[i] for i in candidates]), rest
        for i in candidates:
            addition = min(most - holding[i], max(1, remaining * portions[i] // whole), rest)
            holding[i] = holding[i] + addition
            rest = rest - addition
    return np.array([most] + holding)


def ragged(key, amount, total, bound, slope):
    if amount == 2:
        one = jax.random.randint(key, (), max(1, total - bound), min(bound, total - 1) + 1)
        return jnp.stack([one, total - one])
    sizes = jnp.asarray(split_up(amount, total, bound, slope), jnp.int32)
    twos = (amount - 1) // 2
    source_of, receiver = sizes[1:1 + 2 * twos:2], sizes[2:2 + 2 * twos:2]
    margin = jnp.minimum(source_of - 1, bound - receiver)
    shifted = jax.random.randint(jax.random.fold_in(key, 1), (twos,), 0, 1 << 20) % (margin + 1)
    sizes = sizes.at[1:1 + 2 * twos:2].set(source_of - shifted).at[2:2 + 2 * twos:2].set(receiver + shifted)
    return sizes[jax.random.permutation(jax.random.fold_in(key, 2), amount)]


def gaussian(stream_key, dims, spread, most, cuts=(), kind=jnp.bfloat16):
    factor_of = level_of(stream_key, dims, cuts, -0.22, 0.18) if cuts else 1.0
    drawn = jax.random.normal(stream_key, dims, jnp.float32) * spread * factor_of
    return jnp.minimum(jnp.maximum(drawn, -most), most).astype(kind)


def setup_inputs(seed: int = 0, part: int = 0) -> dict:
    key_of = jax.random.split(jax.random.key(seed), 14)
    part_splits = jax.random.split(jax.random.fold_in(key_of[13], part), 14)
    return {
        "patches": draw_patches(jax.random.fold_in(jax.random.fold_in(key_of[13], part), 71), part),
        "vit_gain": jnp.clip(1.0 + 0.18 * jax.random.normal(key_of[1], (DV,), jnp.float32), 0.1, 1.9),
        "vit_fc1": gaussian(key_of[2], (DV, FFV), DV ** -0.5, 0.109375, ((1, 16),)),
        "vit_fc2": gaussian(key_of[3], (FFV, DV), FFV ** -0.5, 0.0546875, ((0, 16),)),
        "proj_gain": jnp.clip(1.0 + 0.18 * jax.random.normal(key_of[4], (SHUF * DV,), jnp.float32), 0.1, 1.9),
        "proj_bias": gaussian(key_of[5], (SHUF * DV,), 0.5, 3.0, (), jnp.float32),
        "proj_weight": gaussian(key_of[6], (SHUF * DV, D), (SHUF * DV) ** -0.5, 0.0546875, ((1, 16),)),
        "llm_gain": jnp.clip(1.0 + 0.18 * jax.random.normal(key_of[7], (D,), jnp.float32), 0.1, 1.9),
        "qkv_weight": gaussian(key_of[8], (D, QKVW), D ** -0.5, 0.0625, ((0, 16),)),
        "text_query": draw_text_query(jax.random.fold_in(jax.random.fold_in(key_of[13], part), 71), part),
        "text_keyvalue": draw_text_keyvalue(jax.random.fold_in(jax.random.fold_in(key_of[13], part), 71), part),
        "doc_ids": jnp.searchsorted(jnp.cumsum(ragged(part_splits[11], 4, SEQ, SEQ * 5 // 8, 0)), jnp.arange(SEQ), side="right").astype(jnp.int32),
        "image_positions": draw_image_positions(jax.random.fold_in(jax.random.fold_in(key_of[13], part), 71), part),
    }


def rotate(rows, positions):
    row_count = rows.shape[0]
    half_dim = HD // 2
    inv_freq = 1000000.0 ** (-2.0 * jnp.arange(half_dim, dtype=jnp.float32) / HD)
    angles = positions.astype(jnp.float32)[:, None] * inv_freq[None, :]
    cosine = jnp.cos(angles)[:, None, :]
    sine_part = jnp.sin(angles)[:, None, :]

    def rotate_part(part, head_count):
        head_grid = part.reshape(row_count, head_count, HD)
        lower = head_grid[..., :half_dim]
        upper = head_grid[..., half_dim:]
        turned = jnp.concatenate([lower * cosine - upper * sine_part, upper * cosine + lower * sine_part], axis=-1)
        return turned.reshape(row_count, head_count * HD)
    query_part = rotate_part(rows[:, :QH * HD], QH)
    key_part = rotate_part(rows[:, QH * HD:(QH + KVH) * HD], KVH)
    return jnp.concatenate([query_part, key_part, rows[:, (QH + KVH) * HD:]], axis=1)

def reference(patches, vit_gain, vit_fc1, vit_fc2, proj_gain, proj_bias, proj_weight, llm_gain, qkv_weight, text_query, text_keyvalue, doc_ids, image_positions):
    values = patches.astype(jnp.float32)
    vit_norm = (values * lax.rsqrt(lax.optimization_barrier(jnp.mean(values * values, axis=-1, keepdims=True)) + 1e-06) * vit_gain).astype(jnp.bfloat16)
    vit_hidden = jax.nn.gelu(jnp.dot(vit_norm, vit_fc1, preferred_element_type=jnp.float32), approximate=False).astype(jnp.bfloat16)
    vit_out = (values + jnp.dot(vit_hidden, vit_fc2, preferred_element_type=jnp.float32)).astype(jnp.bfloat16)
    shuffled = vit_out.reshape(IMG, SHUF * DV).astype(jnp.float32)
    row_mean = lax.optimization_barrier(jnp.mean(shuffled, axis=-1, keepdims=True))
    centre = shuffled - row_mean
    variance = lax.optimization_barrier(jnp.mean(centre * centre, axis=-1, keepdims=True))
    proj_norm = (centre * lax.rsqrt(variance + 1e-05) * proj_gain + proj_bias).astype(jnp.bfloat16)
    projected = jax.nn.gelu(jnp.dot(proj_norm, proj_weight, preferred_element_type=jnp.float32), approximate=False).astype(jnp.bfloat16)
    proj_float = projected.astype(jnp.float32)
    inv_rms = lax.rsqrt(lax.optimization_barrier(jnp.sum(proj_float * proj_float, axis=-1)) / D + 1e-06)
    llm_norm = (proj_float * inv_rms[:, None] * llm_gain).astype(jnp.bfloat16)
    image_qkv = jnp.dot(llm_norm, qkv_weight, preferred_element_type=jnp.float32)
    image_rows = rotate(image_qkv, image_positions).astype(jnp.bfloat16)
    query = text_query.at[image_positions].set(image_rows[:, :QH * HD])
    keyvalue = text_keyvalue.at[image_positions].set(image_rows[:, QH * HD:])
    group = QH // KVH
    scale = HD ** (-0.5)
    key_rows = keyvalue[:, :KVH * HD].reshape(SEQ, KVH, HD).astype(jnp.float32)
    value_rows = keyvalue[:, KVH * HD:].reshape(SEQ, KVH, HD).astype(jnp.float32)
    block_size = min(512, SEQ)
    query_grid = query.reshape(SEQ // block_size, block_size, KVH, group, HD)
    positions = jnp.arange(SEQ, dtype=jnp.int32)

    def attend(inputs_tuple):
        query_block, query_pos, query_doc = inputs_tuple
        allowed = (positions[None, :] <= query_pos[:, None]) & (doc_ids[None, :] == query_doc[:, None])

        def head_attend(head_inputs):
            query_head, key_head, value_head = head_inputs
            scores = jnp.einsum('qmd,kd->mqk', query_head.astype(jnp.float32), key_head) * scale
            scores = jnp.where(allowed[None], scores, -jnp.inf)
            row_max = lax.optimization_barrier(jnp.max(scores, axis=-1, keepdims=True))
            weights = jnp.where(allowed[None], jnp.exp(scores - row_max), 0.0)
            rounded = lax.optimization_barrier(weights.astype(jnp.bfloat16)).astype(jnp.float32)
            context = jnp.einsum('mqk,kd->qmd', rounded, value_head)
            return context / jnp.transpose(lax.optimization_barrier(jnp.sum(weights, axis=-1)))[:, :, None]
        head_outs = lax.map(head_attend, (jnp.transpose(query_block, (1, 0, 2, 3)), jnp.transpose(key_rows, (1, 0, 2)), jnp.transpose(value_rows, (1, 0, 2))))
        return jnp.transpose(head_outs, (1, 0, 2, 3)).reshape(block_size, QH * HD).astype(jnp.bfloat16)
    block_outs = lax.map(attend, (query_grid, positions.reshape(-1, block_size), doc_ids.reshape(-1, block_size)))
    return block_outs.reshape(SEQ, QH * HD)
```

```python
import functools
import jax
import jax.numpy as jnp
from jax import lax
from jax.experimental import pallas as pl
from jax.experimental.pallas import tpu as pltpu
from jax.sharding import PartitionSpec as P

DV = 3200
SHUF = 4
D = 8192
QH = 64
KVH = 8
HD = 128
ROWW = 2560
EXT = 128
F32 = jnp.float32
BF16 = jnp.bfloat16


def gelu(x):
    return 0.5 * x * (1.0 + lax.erf(x * (2.0 ** -0.5)))


def narrow_plain(dst, v):
    dst[...] = v.astype(BF16)


def two_parts(total):
    lane = lax.broadcasted_iota(jnp.int32, (total.shape[0], EXT), 1)
    high = total.astype(BF16).astype(F32)
    return jnp.where(lane == 0, high, jnp.where(lane == 1, total - high, 0.0))


def narrow_ext(dst, v):
    dst[:, :ROWW] = v[:, :ROWW].astype(BF16)
    dst[:, ROWW:] = two_parts(jnp.sum(v[:, ROWW:], axis=1, keepdims=True)).astype(BF16)


def image_kernel(
    n,
    patches,
    vit_gain,
    fc1_hbm,
    fc2_hbm,
    proj_gain,
    proj_bias,
    proj_hbm,
    llm_gain,
    qkv_hbm,
    turn,
    out,
    fc1,
    fc2,
    proj,
    qkv,
    g1, g2, g3,
    b1, r1a, a1b, r1b, a1c, r1c,
    b2, r2a, a2b, r2b, a2c, r2c,
    work,
    lhs,
    hid_acc,
    hidden,
    proj_acc,
    wsem,
    ag_send, ag_recv,
    rs_send, rs_recv,
):
    Z = n // 4
    group = lax.axis_index("groups")
    me = lax.axis_index("ctx")
    z, y, c = me // 4, lax.rem(me // 2, 2), lax.rem(me, 2)

    def dev(zz, yy, cc):
        return (group, zz * 4 + yy * 2 + cc)

    zs = [lax.rem(z + k, Z) for k in range(Z)]
    zr = [lax.rem(z + Z - k, Z) for k in range(Z)]
    ydev, cdev = dev(z, 1 - y, c), dev(z, y, 1 - c)
    own = (c * 2 + y) * Z
    own_y = (c * 2 + 1 - y) * Z
    slot = own + z

    loads = [pltpu.make_async_copy(fc1_hbm, fc1, wsem.at[0]),
             pltpu.make_async_copy(fc2_hbm, fc2, wsem.at[1])]
    for r in range(SHUF):
        loads.append(pltpu.make_async_copy(
            proj_hbm.at[pl.ds(r * DV, DV)], proj.at[pl.ds(r * DV, DV)], wsem.at[2 + r]))
    loads.append(pltpu.make_async_copy(qkv_hbm, qkv, wsem.at[2 + SHUF]))
    for load in loads:
        load.start()

    barrier = pltpu.get_barrier_semaphore()
    partners = [dev(zs[k], y, c) for k in range(1, Z)] + [ydev, cdev]
    for partner in partners:
        pl.semaphore_signal(barrier, inc=1, device_id=partner, device_id_type=pl.DeviceIdType.MESH)
    pl.semaphore_wait(barrier, len(partners))

    def remote(src, dst, ss, rs, to):
        return pltpu.make_async_remote_copy(
            src_ref=src, dst_ref=dst, send_sem=ss, recv_sem=rs,
            device_id=to, device_id_type=pl.DeviceIdType.MESH)

    def gather(buf, which):
        ss, rs = ag_send.at[which], ag_recv.at[which]
        sent = []

        def send(at, sem, to):
            copy = remote(buf.at[at], buf.at[at], ss.at[sem], rs.at[sem], to)
            copy.start()
            sent.append(copy)

        def arrived(at, sem):
            remote(buf.at[at], buf.at[at], ss.at[sem], rs.at[sem], cdev).wait_recv()

        for k in range(1, Z):
            send(slot, k, dev(zs[k], y, c))
        send(slot, Z, ydev)
        send(slot, 2 * Z, cdev)
        for k in range(1, Z):
            arrived(own + zr[k], k)
            send(own + zr[k], Z + k, ydev)
            send(own + zr[k], 2 * Z + k, cdev)
        for k in range(Z):
            arrived(own_y + zr[k], Z + k)
            send(own_y + zr[k], 3 * Z + k, cdev)
        other = ((1 - c) * 2 + y) * Z
        other_y = ((1 - c) * 2 + 1 - y) * Z
        for k in range(Z):
            arrived(other + zr[k], 2 * Z + k)
        for k in range(Z):
            arrived(other_y + zr[k], 3 * Z + k)
        return sent

    def reduce(buf, ra, ab, rb, ac, rc, which, narrow):
        ss, rs = rs_send.at[which], rs_recv.at[which]
        sent = []

        def send(src, dst, sem, to):
            copy = remote(src, dst, ss.at[sem], rs.at[sem], to)
            copy.start()
            sent.append(copy)

        def arrived(dst, sem):
            remote(dst, dst, ss.at[sem], rs.at[sem], cdev).wait_recv()

        for half in range(2):
            yy = (1 - y) if half == 0 else y
            send(buf.at[pl.ds(((1 - c) * 2 + yy) * Z, Z)], ra.at[half], half, cdev)
        arrived(ra.at[0], 0)
        order = list(range(1, Z)) + [0]
        for k in order:
            narrow(ab.at[k], buf[own_y + zs[k]].astype(F32) + ra[0, zs[k]].astype(F32))
            send(ab.at[k], rb.at[k], 2 + k, ydev)
        arrived(ra.at[1], 1)
        total = None
        for k in order:
            arrived(rb.at[k], 2 + k)
            mine = (buf[own + zs[k]].astype(F32) + ra[1, zs[k]].astype(F32)) + rb[k].astype(F32)
            if k == 0:
                total = mine
            else:
                narrow(ac.at[k], mine)
                send(ac.at[k], rc.at[k], Z + 2 + k, dev(zs[k], y, c))
        for k in range(1, Z):
            arrived(rc.at[k], Z + 2 + k)
            total = total + rc[k].astype(F32)
        return total, sent

    def unpack(buf, width, place=lambda i: i):
        for i in range(n):
            v = buf[i].astype(F32)
            for j in range(width // 128):
                work[j, pl.ds(4 * place(i), 4), :] = v[:, j * 128:(j + 1) * 128]

    def pack(buf, width):
        for i in range(n):
            for j in range(width // 128):
                buf[i, :, pl.ds(j * 128, 128)] = work[j, pl.ds(4 * i, 4), :].astype(BF16)

    values = patches[...].astype(F32)
    mean_sq = jnp.mean(values * values, axis=-1, keepdims=True)
    g1[slot] = (values * lax.rsqrt(mean_sq + 1e-6) * vit_gain[...]).astype(BF16)
    sends = gather(g1, 0)

    unpack(g1, DV)
    for j in range(DV // 128):
        lhs[:, pl.ds(j * 128, 128)] = work[j].astype(BF16)
    loads[0].wait()
    hid_acc[...] = jnp.zeros_like(hid_acc)

    @pl.loop(0, DV // 640)
    def _(j):
        at = pl.ds(pl.multiple_of(j * 640, 128), 640)
        hid_acc[...] += jnp.dot(lhs[:, at], fc1[at, :], preferred_element_type=F32)

    hidden[...] = gelu(hid_acc[...]).astype(BF16)
    loads[1].wait()

    @pl.loop(0, DV // 640)
    def _(j):
        at = pl.ds(pl.multiple_of(j * 640, 128), 640)
        part = jnp.dot(hidden[...], fc2[:, at], preferred_element_type=F32)
        for m in range(5):
            work[j * 5 + m] = part[:, m * 128:(m + 1) * 128]

    pack(b1, DV)
    total, more = reduce(b1, r1a, a1b, r1b, a1c, r1c, 0, narrow_plain)
    sends += more
    shuffled = (patches[...].astype(F32) + total).astype(BF16).astype(F32)
    row_mean = jnp.sum(jnp.sum(shuffled, axis=1, keepdims=True), axis=0, keepdims=True) / (SHUF * DV)
    centre = shuffled - row_mean
    var = jnp.sum(jnp.sum(centre * centre, axis=1, keepdims=True), axis=0, keepdims=True) / (SHUF * DV)
    g2[slot] = (centre * lax.rsqrt(var + 1e-5) * proj_gain[...] + proj_bias[...]).astype(BF16)
    sends += gather(g2, 1)

    unpack(g2, DV)
    proj_acc[...] = jnp.zeros_like(proj_acc)
    for r in range(SHUF):
        loads[2 + r].wait()
        lhs[:n, :] = jnp.concatenate(
            [work[j, pl.ds(r, n, stride=4), :] for j in range(DV // 128)], axis=1
        ).astype(BF16)

        @pl.loop(0, DV // 640)
        def _(j):
            at = pl.ds(pl.multiple_of(j * 640, 128), 640)
            rows = pl.ds(pl.multiple_of(r * DV + j * 640, 128), 640)
            proj_acc[...] += jnp.dot(lhs[:n, at], proj[rows, :], preferred_element_type=F32)

    projected = gelu(proj_acc[...]).astype(BF16).astype(F32)
    squares = two_parts(jnp.sum(projected * projected, axis=1, keepdims=True))
    scaled = (projected * llm_gain[...]).astype(BF16)
    loads[2 + SHUF].wait()
    for r in range(SHUF):
        for j in range(ROWW // 640):
            part = jnp.dot(scaled, qkv[:, pl.ds(r * ROWW + j * 640, 640)], preferred_element_type=F32)
            for m in range(5):
                work[j * 5 + m, pl.ds(r, n, stride=4), :] = part[:, m * 128:(m + 1) * 128]
        work[ROWW // 128, pl.ds(r, n, stride=4), :] = squares
    pack(b2, ROWW + EXT)
    total, more = reduce(b2, r2a, a2b, r2b, a2c, r2c, 1, narrow_ext)
    sends += more
    square_sum = jnp.sum(total[:, ROWW:], axis=1, keepdims=True)
    inv_rms = lax.rsqrt(square_sum / D + 1e-6)
    cosine, sine = turn[0:1, :], turn[1:2, :]
    row = lax.broadcasted_iota(jnp.int32, (SHUF, HD), 0)
    for h in range(ROWW // HD):
        x = total[:, h * HD:(h + 1) * HD] * inv_rms
        turned = x * cosine + pltpu.roll(x, HD // 2, 1) * sine
        g3[slot, :, pl.ds(h * HD, HD)] = jnp.where(
            row * (ROWW // HD) + h < QH + KVH, turned, x).astype(BF16)
    sends += gather(g3, 2)
    unpack(g3, ROWW, lambda i: (i % Z) * 4 + (i // Z) % 2 * 2 + i // (2 * Z))
    for r in range(SHUF):
        for j in range(ROWW // HD):
            out[:, pl.ds(r * ROWW + j * HD, HD)] = work[j, pl.ds(r, n, stride=4), :].astype(BF16)
    for copy in sends:
        copy.wait_send()


def image_rows(n, patches, vit_gain, fc1, fc2, proj_gain, proj_bias, proj, llm_gain, qkv, turn):
    Z = n // 4
    vm = pl.BlockSpec(memory_space=pltpu.VMEM)
    hbm = pl.BlockSpec(memory_space=pl.ANY)

    def reduce_bufs(width):
        return [
            pltpu.VMEM((n, SHUF, width), BF16),
            pltpu.VMEM((2, Z, SHUF, width), BF16),
        ] + [pltpu.VMEM((Z, SHUF, width), BF16)] * 4

    hid = fc1.shape[1]
    cols = proj.shape[1]
    weights = sum(w.size for w in (fc1, fc2, proj, qkv))
    return pl.pallas_call(
        functools.partial(image_kernel, n),
        out_shape=jax.ShapeDtypeStruct((n, SHUF * ROWW), BF16),
        in_specs=[vm, vm, hbm, hbm, vm, vm, hbm, vm, hbm, vm],
        out_specs=vm,
        scratch_shapes=[
            pltpu.VMEM(fc1.shape, BF16),
            pltpu.VMEM(fc2.shape, BF16),
            pltpu.VMEM(proj.shape, BF16),
            pltpu.VMEM(qkv.shape, BF16),
            pltpu.VMEM((n, SHUF, DV), BF16),
            pltpu.VMEM((n, SHUF, DV), BF16),
            pltpu.VMEM((n, SHUF, ROWW), BF16),
        ] + reduce_bufs(DV) + reduce_bufs(ROWW + EXT) + [
            pltpu.VMEM((DV // 128, n * SHUF, 128), F32),
            pltpu.VMEM((n * SHUF, DV), BF16),
            pltpu.VMEM((n * SHUF, hid), F32),
            pltpu.VMEM((n * SHUF, hid), BF16),
            pltpu.VMEM((n, cols), F32),
            pltpu.SemaphoreType.DMA((3 + SHUF,)),
            pltpu.SemaphoreType.DMA((3, 4 * Z)),
            pltpu.SemaphoreType.DMA((3, 4 * Z)),
            pltpu.SemaphoreType.DMA((2, 2 * Z + 2)),
            pltpu.SemaphoreType.DMA((2, 2 * Z + 2)),
        ],
        compiler_params=pltpu.CompilerParams(
            collective_id=0, has_side_effects=True, vmem_limit_bytes=56 * 2 ** 20),
        cost_estimate=pl.CostEstimate(
            flops=64 * weights, bytes_accessed=2 * weights, transcendentals=0),
    )(patches, vit_gain, fc1, fc2, proj_gain, proj_bias, proj, llm_gain, qkv, turn)


def attend_kernel(n, span, width, query, keys, vals, doc, pos, iq, ik, iv, out, bias, hit_k, img_k, hit_q, img_q):
    rows = query.shape[0]
    me = lax.axis_index("ctx")
    first = jnp.clip(lax.div(jnp.maximum(me - span, 0), 2) * 2, 0, n - width // rows) * rows
    first = pl.multiple_of(first, 2 * rows)
    group = QH // KVH

    @pl.when(pl.program_id(0) == 0)
    def _():
        docs = doc[...]
        q_pos = me * rows + lax.broadcasted_iota(jnp.int32, (rows, docs.shape[1]), 0)
        k_pos = lax.broadcasted_iota(jnp.int32, (rows, docs.shape[1]), 1)
        q_doc = jnp.sum(jnp.where(q_pos == k_pos, docs, 0), axis=1, keepdims=True)
        k_doc = doc[:, pl.ds(first, width)]
        ok = (first + k_pos[:, :width] <= q_pos[:, :width]) & (k_doc == q_doc)
        bias[...] = jnp.where(ok, 0.0, -1e30)

        def hits(count, start):
            at = start + lax.broadcasted_iota(jnp.int32, (count, n), 0)
            hit = (at == pos[...]).astype(F32)
            return hit.astype(BF16), jnp.sum(hit, axis=1, keepdims=True)

        table, live = hits(width, first)
        hit_k[...] = table
        img_k[...] = jnp.broadcast_to(live, img_k.shape)
        table, live = hits(rows, me * rows)
        hit_q[...] = table
        img_q[...] = jnp.broadcast_to(live, img_q.shape)

    def put(live, table, image, text):
        placed = jnp.dot(table, image, preferred_element_type=F32)
        return jnp.where(live > 0.0, placed, text.astype(F32)).astype(BF16)

    k = put(img_k[...], hit_k[...], ik[...], keys[pl.ds(first, width), :])
    v = put(img_k[...], hit_k[...], iv[...], vals[pl.ds(first, width), :])
    scale = HD ** -0.5
    for m in range(group):
        at = slice(m * HD, (m + 1) * HD)
        q = put(img_q[...], hit_q[...], iq[:, at], query[:, at])
        s = lax.dot_general(q, k, (((1,), (1,)), ((), ())), preferred_element_type=F32)
        s = s * scale + bias[...]
        w = jnp.exp(s - jnp.max(s, axis=1, keepdims=True))
        total = jnp.sum(w, axis=1, keepdims=True)
        o = jnp.dot(w.astype(BF16), v, preferred_element_type=F32)
        out[:, at] = (o / total).astype(BF16)


def attention(n, query, keyvalue, doc, pos, image):
    rows = query.shape[0]
    seq = keyvalue.shape[0]
    group = QH // KVH
    span = seq * 5 // 8 // rows
    width = min(span + 2, n) * rows
    return pl.pallas_call(
        functools.partial(attend_kernel, n, span, width),
        grid=(KVH,),
        out_shape=jax.ShapeDtypeStruct((rows, QH * HD), BF16),
        in_specs=[
            pl.BlockSpec((rows, group * HD), lambda g: (0, g)),
            pl.BlockSpec((seq, HD), lambda g: (0, g)),
            pl.BlockSpec((seq, HD), lambda g: (0, KVH + g)),
            pl.BlockSpec((1, seq), lambda g: (0, 0)),
            pl.BlockSpec((1, n), lambda g: (0, 0)),
            pl.BlockSpec((n, group * HD), lambda g: (0, g)),
            pl.BlockSpec((n, HD), lambda g: (0, QH + g)),
            pl.BlockSpec((n, HD), lambda g: (0, QH + KVH + g)),
        ],
        out_specs=pl.BlockSpec((rows, group * HD), lambda g: (0, g)),
        scratch_shapes=[
            pltpu.VMEM((rows, width), F32),
            pltpu.VMEM((width, n), BF16),
            pltpu.VMEM((width, HD), F32),
            pltpu.VMEM((rows, n), BF16),
            pltpu.VMEM((rows, HD), F32),
        ],
        compiler_params=pltpu.CompilerParams(vmem_limit_bytes=48 * 2 ** 20),
        cost_estimate=pl.CostEstimate(
            flops=4 * rows * QH * HD * width, bytes_accessed=4 * query.size + 2 * keyvalue.size,
            transcendentals=rows * QH * width),
    )(query, keyvalue, keyvalue, doc, pos, image, image, image)


def shards(
    n,
    patches,
    vit_gain,
    vit_fc1,
    vit_fc2,
    proj_gain,
    proj_bias,
    proj_weight,
    llm_gain,
    qkv_weight,
    text_query,
    text_keyvalue,
    doc_ids,
    image_positions,
):
    kv_all = lax.all_gather(text_keyvalue, "ctx", axis=0, tiled=True)
    doc_all = lax.all_gather(doc_ids, "ctx", axis=0, tiled=True)
    half = HD // 2
    inv_freq = 1000000.0 ** (-2.0 * jnp.arange(half, dtype=F32) / HD)
    own_pos = lax.dynamic_index_in_dim(image_positions, lax.axis_index("ctx"), 0, keepdims=False)
    angle = own_pos.astype(F32) * inv_freq
    cosine, sine = jnp.cos(angle), jnp.sin(angle)
    turn = jnp.stack([jnp.concatenate([cosine, cosine]), jnp.concatenate([-sine, sine])])
    image = image_rows(
        n, patches, vit_gain.reshape(1, DV), vit_fc1, vit_fc2,
        proj_gain.reshape(SHUF, DV), proj_bias.reshape(SHUF, DV), proj_weight,
        llm_gain.reshape(1, -1), qkv_weight, turn)
    return attention(
        n, text_query, kv_all, doc_all.reshape(1, -1), image_positions.reshape(1, -1), image)


def solution(mesh):
    placed = (
        P(("groups", "ctx"), None),
        P(),
        P(None, "ctx"),
        P("ctx", None),
        P(),
        P(),
        P(None, "ctx"),
        P("ctx"),
        P("ctx", None),
        P(("groups", "ctx"), None),
        P(("groups", "ctx"), None),
        P(("groups", "ctx")),
        P("groups"),
    )
    return jax.shard_map(
        functools.partial(shards, mesh.shape["ctx"]), mesh=mesh, in_specs=placed,
        out_specs=P(("groups", "ctx"), None), check_vma=False)
```

```python
import functools
import jax
import jax.numpy as jnp
from jax import lax
from jax.experimental import pallas as pl
from jax.experimental.pallas import tpu as pltpu
from jax.sharding import PartitionSpec as P

DV = 3200
SHUF = 4
D = 8192
QH = 64
KVH = 8
HD = 128
ROWW = 2560
EXT = 128
F32 = jnp.float32
BF16 = jnp.bfloat16


def gelu(x):
    return 0.5 * x * (1.0 + lax.erf(x * (2.0 ** -0.5)))


def narrow_plain(dst, v):
    dst[...] = v.astype(BF16)


def two_parts(total):
    lane = lax.broadcasted_iota(jnp.int32, (total.shape[0], EXT), 1)
    high = total.astype(BF16).astype(F32)
    return jnp.where(lane == 0, high, jnp.where(lane == 1, total - high, 0.0))


def narrow_ext(dst, v):
    dst[:, :ROWW] = v[:, :ROWW].astype(BF16)
    dst[:, ROWW:] = two_parts(jnp.sum(v[:, ROWW:], axis=1, keepdims=True)).astype(BF16)


def image_kernel(
    n,
    patches,
    vit_gain,
    fc1_hbm,
    fc2_hbm,
    proj_gain,
    proj_bias,
    proj_hbm,
    llm_gain,
    qkv_hbm,
    turn,
    doc,
    out,
    doc_out,
    fc1,
    fc2,
    proj,
    qkv,
    g1, g2, g3,
    b1, r1a, a1b, r1b, a1c, r1c,
    b2, r2a, a2b, r2b, a2c, r2c,
    work,
    lhs,
    hid_acc,
    hidden,
    proj_acc,
    wsem,
    ag_send, ag_recv,
    rs_send, rs_recv,
):
    Z = n // 4
    group = lax.axis_index("groups")
    me = lax.axis_index("ctx")
    z, y, c = me // 4, lax.rem(me // 2, 2), lax.rem(me, 2)

    def dev(zz, yy, cc):
        return (group, zz * 4 + yy * 2 + cc)

    zs = [lax.rem(z + k, Z) for k in range(Z)]
    zr = [lax.rem(z + Z - k, Z) for k in range(Z)]
    ydev, cdev = dev(z, 1 - y, c), dev(z, y, 1 - c)
    own = (c * 2 + y) * Z
    own_y = (c * 2 + 1 - y) * Z
    slot = own + z

    loads = [pltpu.make_async_copy(fc1_hbm, fc1, wsem.at[0]),
             pltpu.make_async_copy(fc2_hbm, fc2, wsem.at[1])]
    for r in range(SHUF):
        loads.append(pltpu.make_async_copy(
            proj_hbm.at[pl.ds(r * DV, DV)], proj.at[pl.ds(r * DV, DV)], wsem.at[2 + r]))
    loads.append(pltpu.make_async_copy(qkv_hbm, qkv, wsem.at[2 + SHUF]))
    for load in loads:
        load.start()

    barrier = pltpu.get_barrier_semaphore()
    partners = [dev(zs[k], y, c) for k in range(1, Z)] + [ydev, cdev]
    for partner in partners:
        pl.semaphore_signal(barrier, inc=1, device_id=partner, device_id_type=pl.DeviceIdType.MESH)
    pl.semaphore_wait(barrier, len(partners))

    def remote(src, dst, ss, rs, to):
        return pltpu.make_async_remote_copy(
            src_ref=src, dst_ref=dst, send_sem=ss, recv_sem=rs,
            device_id=to, device_id_type=pl.DeviceIdType.MESH)

    def gather(buf, which):
        ss, rs = ag_send.at[which], ag_recv.at[which]
        sent = []

        def send(at, sem, to):
            copy = remote(buf.at[at], buf.at[at], ss.at[sem], rs.at[sem], to)
            copy.start()
            sent.append(copy)

        def arrived(at, sem):
            remote(buf.at[at], buf.at[at], ss.at[sem], rs.at[sem], cdev).wait_recv()

        for k in range(1, Z):
            send(slot, k, dev(zs[k], y, c))
        send(slot, Z, ydev)
        send(slot, 2 * Z, cdev)
        for k in range(1, Z):
            arrived(own + zr[k], k)
            send(own + zr[k], Z + k, ydev)
            send(own + zr[k], 2 * Z + k, cdev)
        for k in range(Z):
            arrived(own_y + zr[k], Z + k)
            send(own_y + zr[k], 3 * Z + k, cdev)
        other = ((1 - c) * 2 + y) * Z
        other_y = ((1 - c) * 2 + 1 - y) * Z
        for k in range(Z):
            arrived(other + zr[k], 2 * Z + k)
        for k in range(Z):
            arrived(other_y + zr[k], 3 * Z + k)
        return sent

    def reduce(buf, ra, ab, rb, ac, rc, which, narrow):
        ss, rs = rs_send.at[which], rs_recv.at[which]
        sent = []

        def send(src, dst, sem, to):
            copy = remote(src, dst, ss.at[sem], rs.at[sem], to)
            copy.start()
            sent.append(copy)

        def arrived(dst, sem):
            remote(dst, dst, ss.at[sem], rs.at[sem], cdev).wait_recv()

        for half in range(2):
            yy = (1 - y) if half == 0 else y
            send(buf.at[pl.ds(((1 - c) * 2 + yy) * Z, Z)], ra.at[half], half, cdev)
        arrived(ra.at[0], 0)
        order = list(range(1, Z)) + [0]
        for k in order:
            narrow(ab.at[k], buf[own_y + zs[k]].astype(F32) + ra[0, zs[k]].astype(F32))
            send(ab.at[k], rb.at[k], 2 + k, ydev)
        arrived(ra.at[1], 1)
        total = None
        for k in order:
            arrived(rb.at[k], 2 + k)
            mine = (buf[own + zs[k]].astype(F32) + ra[1, zs[k]].astype(F32)) + rb[k].astype(F32)
            if k == 0:
                total = mine
            else:
                narrow(ac.at[k], mine)
                send(ac.at[k], rc.at[k], Z + 2 + k, dev(zs[k], y, c))
        for k in range(1, Z):
            arrived(rc.at[k], Z + 2 + k)
            total = total + rc[k].astype(F32)
        return total, sent

    def unpack(buf, width, place=lambda i: i):
        for i in range(n):
            v = buf[i].astype(F32)
            for j in range(width // 128):
                work[j, pl.ds(4 * place(i), 4), :] = v[:, j * 128:(j + 1) * 128]

    def pack(buf, width):
        for i in range(n):
            for j in range(width // 128):
                buf[i, :, pl.ds(j * 128, 128)] = work[j, pl.ds(4 * i, 4), :].astype(BF16)

    values = patches[...].astype(F32)
    mean_sq = jnp.mean(values * values, axis=-1, keepdims=True)
    g1[slot, :, pl.ds(DV, EXT)] = doc[...]
    g1[slot, :, pl.ds(0, DV)] = (values * lax.rsqrt(mean_sq + 1e-6) * vit_gain[...]).astype(BF16)
    sends = gather(g1, 0)

    unpack(g1, DV + EXT)
    lane = lax.broadcasted_iota(jnp.int32, (1, 128), 1)
    for m in range(n // 2):
        low, high = [
            work[DV // 128, pl.ds(4 * (((i % 2) * 2 + (i // 2) % 2) * Z + i // 4), 1), :]
            for i in (2 * m, 2 * m + 1)]
        doc_out[:, pl.ds(m * 128, 128)] = jnp.where(lane < 64, low, pltpu.roll(high, 64, 1))
    for j in range(DV // 128):
        lhs[:, pl.ds(j * 128, 128)] = work[j].astype(BF16)
    loads[0].wait()
    hid_acc[...] = jnp.zeros_like(hid_acc)

    @pl.loop(0, DV // 640)
    def _(j):
        at = pl.ds(pl.multiple_of(j * 640, 128), 640)
        hid_acc[...] += lax.dot_general(
            lhs[:, at], fc1[:, at], (((1,), (1,)), ((), ())), preferred_element_type=F32)

    hidden[...] = gelu(hid_acc[...]).astype(BF16)
    loads[1].wait()

    @pl.loop(0, DV // 640)
    def _(j):
        at = pl.ds(pl.multiple_of(j * 640, 128), 640)
        part = jnp.dot(hidden[...], fc2[:, at], preferred_element_type=F32)
        for m in range(5):
            work[j * 5 + m] = part[:, m * 128:(m + 1) * 128]

    pack(b1, DV)
    total, more = reduce(b1, r1a, a1b, r1b, a1c, r1c, 0, narrow_plain)
    sends += more
    shuffled = (patches[...].astype(F32) + total).astype(BF16).astype(F32)
    row_mean = jnp.sum(jnp.sum(shuffled, axis=1, keepdims=True), axis=0, keepdims=True) / (SHUF * DV)
    centre = shuffled - row_mean
    var = jnp.sum(jnp.sum(centre * centre, axis=1, keepdims=True), axis=0, keepdims=True) / (SHUF * DV)
    g2[slot] = (centre * lax.rsqrt(var + 1e-5) * proj_gain[...] + proj_bias[...]).astype(BF16)
    sends += gather(g2, 1)

    unpack(g2, DV)
    proj_acc[...] = jnp.zeros_like(proj_acc)
    for r in range(SHUF):
        loads[2 + r].wait()
        lhs[:n, :] = jnp.concatenate(
            [work[j, pl.ds(r, n, stride=4), :] for j in range(DV // 128)], axis=1
        ).astype(BF16)

        @pl.loop(0, DV // 640)
        def _(j):
            at = pl.ds(pl.multiple_of(j * 640, 128), 640)
            rows = pl.ds(pl.multiple_of(r * DV + j * 640, 128), 640)
            proj_acc[...] += jnp.dot(lhs[:n, at], proj[rows, :], preferred_element_type=F32)

    projected = gelu(proj_acc[...]).astype(BF16).astype(F32)
    squares = two_parts(jnp.sum(projected * projected, axis=1, keepdims=True))
    scaled = (projected * llm_gain[...]).astype(BF16)
    loads[2 + SHUF].wait()
    for r in range(SHUF):
        for j in range(ROWW // 640):
            part = jnp.dot(scaled, qkv[:, pl.ds(r * ROWW + j * 640, 640)], preferred_element_type=F32)
            for m in range(5):
                work[j * 5 + m, pl.ds(r, n, stride=4), :] = part[:, m * 128:(m + 1) * 128]
        work[ROWW // 128, pl.ds(r, n, stride=4), :] = squares
    pack(b2, ROWW + EXT)
    total, more = reduce(b2, r2a, a2b, r2b, a2c, r2c, 1, narrow_ext)
    sends += more
    square_sum = jnp.sum(total[:, ROWW:], axis=1, keepdims=True)
    inv_rms = lax.rsqrt(square_sum / D + 1e-6)
    cosine, sine = turn[0:1, :], turn[1:2, :]
    row = lax.broadcasted_iota(jnp.int32, (SHUF, HD), 0)
    for h in range(ROWW // HD):
        x = total[:, h * HD:(h + 1) * HD] * inv_rms
        turned = x * cosine + pltpu.roll(x, HD // 2, 1) * sine
        g3[slot, :, pl.ds(h * HD, HD)] = jnp.where(
            row * (ROWW // HD) + h < QH + KVH, turned, x).astype(BF16)
    sends += gather(g3, 2)
    unpack(g3, ROWW, lambda i: (i % Z) * 4 + (i // Z) % 2 * 2 + i // (2 * Z))
    for r in range(SHUF):
        for j in range(ROWW // HD):
            out[:, pl.ds(r * ROWW + j * HD, HD)] = work[j, pl.ds(r, n, stride=4), :].astype(BF16)
    for copy in sends:
        copy.wait_send()


def image_rows(n, patches, vit_gain, fc1, fc2, proj_gain, proj_bias, proj, llm_gain, qkv, turn, doc):
    Z = n // 4
    vm = pl.BlockSpec(memory_space=pltpu.VMEM)
    hbm = pl.BlockSpec(memory_space=pl.ANY)

    def reduce_bufs(width):
        return [
            pltpu.VMEM((n, SHUF, width), BF16),
            pltpu.VMEM((2, Z, SHUF, width), BF16),
        ] + [pltpu.VMEM((Z, SHUF, width), BF16)] * 4

    hid = fc1.shape[0]
    cols = proj.shape[1]
    weights = sum(w.size for w in (fc1, fc2, proj, qkv))
    return pl.pallas_call(
        functools.partial(image_kernel, n),
        out_shape=(
            jax.ShapeDtypeStruct((n, SHUF * ROWW), BF16),
            jax.ShapeDtypeStruct((1, n * HD // 2), F32),
        ),
        in_specs=[vm, vm, hbm, hbm, vm, vm, hbm, vm, hbm, vm, vm],
        out_specs=(vm, vm),
        scratch_shapes=[
            pltpu.VMEM(fc1.shape, BF16),
            pltpu.VMEM(fc2.shape, BF16),
            pltpu.VMEM(proj.shape, BF16),
            pltpu.VMEM(qkv.shape, BF16),
            pltpu.VMEM((n, SHUF, DV + EXT), BF16),
            pltpu.VMEM((n, SHUF, DV), BF16),
            pltpu.VMEM((n, SHUF, ROWW), BF16),
        ] + reduce_bufs(DV) + reduce_bufs(ROWW + EXT) + [
            pltpu.VMEM((DV // 128 + 1, n * SHUF, 128), F32),
            pltpu.VMEM((n * SHUF, DV), BF16),
            pltpu.VMEM((n * SHUF, hid), F32),
            pltpu.VMEM((n * SHUF, hid), BF16),
            pltpu.VMEM((n, cols), F32),
            pltpu.SemaphoreType.DMA((3 + SHUF,)),
            pltpu.SemaphoreType.DMA((3, 4 * Z)),
            pltpu.SemaphoreType.DMA((3, 4 * Z)),
            pltpu.SemaphoreType.DMA((2, 2 * Z + 2)),
            pltpu.SemaphoreType.DMA((2, 2 * Z + 2)),
        ],
        compiler_params=pltpu.CompilerParams(
            collective_id=0, has_side_effects=True, vmem_limit_bytes=56 * 2 ** 20),
        cost_estimate=pl.CostEstimate(
            flops=64 * weights, bytes_accessed=2 * weights, transcendentals=0),
    )(patches, vit_gain, fc1, fc2, proj_gain, proj_bias, proj, llm_gain, qkv, turn, doc)


def attend_kernel(n, span, width, query, keys, vals, doc, pos, iq, ik, iv, out, bias, hit_k, img_k, hit_q, img_q):
    rows = query.shape[0]
    me = lax.axis_index("ctx")
    first = jnp.clip(lax.div(jnp.maximum(me - span, 0), 2) * 2, 0, n - width // rows) * rows
    first = pl.multiple_of(first, 2 * rows)
    group = QH // KVH

    @pl.when(pl.program_id(0) == 0)
    def _():
        docs = doc[...]
        q_pos = me * rows + lax.broadcasted_iota(jnp.int32, (rows, docs.shape[1]), 0)
        k_pos = lax.broadcasted_iota(jnp.int32, (rows, docs.shape[1]), 1)
        q_doc = jnp.sum(jnp.where(q_pos == k_pos, docs, 0.0), axis=1, keepdims=True)
        k_doc = doc[:, pl.ds(first, width)]
        ok = (first + k_pos[:, :width] <= q_pos[:, :width]) & (k_doc == q_doc)
        bias[...] = jnp.where(ok, 0.0, -1e30)

        def hits(count, start):
            at = start + lax.broadcasted_iota(jnp.int32, (count, n), 0)
            hit = (at == pos[...]).astype(F32)
            return hit.astype(BF16), jnp.sum(hit, axis=1, keepdims=True)

        table, live = hits(width, first)
        hit_k[...] = table
        img_k[...] = jnp.broadcast_to(live, img_k.shape)
        table, live = hits(rows, me * rows)
        hit_q[...] = table
        img_q[...] = jnp.broadcast_to(live, img_q.shape)

    def put(live, table, image, text):
        placed = jnp.dot(table, image, preferred_element_type=F32)
        return jnp.where(live > 0.0, placed, text.astype(F32)).astype(BF16)

    k = put(img_k[...], hit_k[...], ik[...], keys[pl.ds(first, width), :])
    v = put(img_k[...], hit_k[...], iv[...], vals[pl.ds(first, width), :])
    scale = HD ** -0.5
    table = jnp.concatenate([bias[...]] * 4, axis=0)
    for m in range(0, group, 4):
        heads = [slice((m + i) * HD, (m + i + 1) * HD) for i in range(4)]
        q = jnp.concatenate(
            [put(img_q[...], hit_q[...], iq[:, at], query[:, at]) for at in heads], axis=0)
        s = lax.dot_general(q, k, (((1,), (1,)), ((), ())), preferred_element_type=F32)
        s = s * scale + table
        w = jnp.exp(s - jnp.max(s, axis=1, keepdims=True))
        total = jnp.sum(w, axis=1, keepdims=True)
        o = (jnp.dot(w.astype(BF16), v, preferred_element_type=F32) / total).astype(BF16)
        for i in range(4):
            out[:, heads[i]] = o[i * rows:(i + 1) * rows]


def attention(n, query, keyvalue, doc, pos, image):
    rows = query.shape[0]
    seq = keyvalue.shape[0]
    group = QH // KVH
    span = seq * 5 // 8 // rows
    width = min(span + 2, n) * rows
    return pl.pallas_call(
        functools.partial(attend_kernel, n, span, width),
        grid=(KVH,),
        out_shape=jax.ShapeDtypeStruct((rows, QH * HD), BF16),
        in_specs=[
            pl.BlockSpec((rows, group * HD), lambda g: (0, g)),
            pl.BlockSpec((seq, HD), lambda g: (0, g)),
            pl.BlockSpec((seq, HD), lambda g: (0, KVH + g)),
            pl.BlockSpec((1, seq), lambda g: (0, 0)),
            pl.BlockSpec((1, n), lambda g: (0, 0)),
            pl.BlockSpec((n, group * HD), lambda g: (0, g)),
            pl.BlockSpec((n, HD), lambda g: (0, QH + g)),
            pl.BlockSpec((n, HD), lambda g: (0, QH + KVH + g)),
        ],
        out_specs=pl.BlockSpec((rows, group * HD), lambda g: (0, g)),
        scratch_shapes=[
            pltpu.VMEM((rows, width), F32),
            pltpu.VMEM((width, n), BF16),
            pltpu.VMEM((width, HD), F32),
            pltpu.VMEM((rows, n), BF16),
            pltpu.VMEM((rows, HD), F32),
        ],
        compiler_params=pltpu.CompilerParams(vmem_limit_bytes=48 * 2 ** 20),
        cost_estimate=pl.CostEstimate(
            flops=4 * rows * QH * HD * width, bytes_accessed=4 * query.size + 2 * keyvalue.size,
            transcendentals=rows * QH * width),
    )(query, keyvalue, keyvalue, doc, pos, image, image, image)


def shards(
    n,
    patches,
    vit_gain,
    vit_fc1,
    vit_fc2,
    proj_gain,
    proj_bias,
    proj_weight,
    llm_gain,
    qkv_weight,
    text_query,
    text_keyvalue,
    doc_ids,
    image_positions,
):
    kv_all = lax.all_gather(text_keyvalue, "ctx", axis=0, tiled=True)
    doc = jnp.pad(doc_ids.astype(BF16)[None, :], ((0, SHUF - 1), (0, HD - doc_ids.shape[0])))
    half = HD // 2
    inv_freq = 1000000.0 ** (-2.0 * jnp.arange(half, dtype=F32) / HD)
    own_pos = lax.dynamic_index_in_dim(image_positions, lax.axis_index("ctx"), 0, keepdims=False)
    angle = own_pos.astype(F32) * inv_freq
    cosine, sine = jnp.cos(angle), jnp.sin(angle)
    turn = jnp.stack([jnp.concatenate([cosine, cosine]), jnp.concatenate([-sine, sine])])
    image, doc_all = image_rows(
        n, patches, vit_gain.reshape(1, DV), vit_fc1.T, vit_fc2,
        proj_gain.reshape(SHUF, DV), proj_bias.reshape(SHUF, DV), proj_weight,
        llm_gain.reshape(1, -1), qkv_weight, turn, doc)
    return attention(
        n, text_query, kv_all, doc_all, image_positions.reshape(1, -1), image)


def solution(mesh):
    placed = (
        P(("groups", "ctx"), None),
        P(),
        P(None, "ctx"),
        P("ctx", None),
        P(),
        P(),
        P(None, "ctx"),
        P("ctx"),
        P("ctx", None),
        P(("groups", "ctx"), None),
        P(("groups", "ctx"), None),
        P(("groups", "ctx")),
        P("groups"),
    )
    return jax.shard_map(
        functools.partial(shards, mesh.shape["ctx"]), mesh=mesh, in_specs=placed,
        out_specs=P(("groups", "ctx"), None), check_vma=False)
```

```python
import functools
import jax
import jax.numpy as jnp
from jax import lax
from jax.experimental import pallas as pl
from jax.experimental.pallas import tpu as pltpu
from jax.sharding import PartitionSpec as P

DV = 3200
SHUF = 4
D = 8192
QH = 64
KVH = 8
HD = 128
ROWW = 2560
EXT = 128
F32 = jnp.float32
BF16 = jnp.bfloat16


def gelu(x):
    return 0.5 * x * (1.0 + lax.erf(x * (2.0 ** -0.5)))


def narrow_plain(dst, v):
    dst[...] = v.astype(BF16)


def two_parts(total):
    lane = lax.broadcasted_iota(jnp.int32, (total.shape[0], EXT), 1)
    high = total.astype(BF16).astype(F32)
    return jnp.where(lane == 0, high, jnp.where(lane == 1, total - high, 0.0))


def narrow_ext(dst, v):
    dst[:, :ROWW] = v[:, :ROWW].astype(BF16)
    dst[:, ROWW:] = two_parts(jnp.sum(v[:, ROWW:], axis=1, keepdims=True)).astype(BF16)


def image_kernel(
    n,
    patches,
    vit_gain,
    fc1_hbm,
    fc2_hbm,
    proj_gain,
    proj_bias,
    proj_hbm,
    llm_gain,
    qkv_hbm,
    cosine,
    sine,
    doc,
    out,
    doc_out,
    fc1,
    fc2,
    proj,
    qkv,
    g1, g2, g3,
    b1, r1a, a1b, r1b, a1c, r1c,
    b2, r2a, a2b, r2b, a2c, r2c,
    work,
    lhs,
    hid_acc,
    hidden,
    proj_acc,
    wsem,
    ag_send, ag_recv,
    rs_send, rs_recv,
):
    Z = n // 4
    group = lax.axis_index("groups")
    me = lax.axis_index("ctx")
    z, y, c = me // 4, lax.rem(me // 2, 2), lax.rem(me, 2)

    def dev(zz, yy, cc):
        return (group, zz * 4 + yy * 2 + cc)

    if Z & (Z - 1):
        zs = [lax.rem(z + k, Z) for k in range(Z)]
        zr = [lax.rem(z + Z - k, Z) for k in range(Z)]
    else:

        def flipped(k):
            at = z
            for b in range(k.bit_length()):
                if (k >> b) & 1:
                    at = at + 2 ** b - 2 ** (b + 1) * lax.rem(z // 2 ** b, 2)
            return at

        zs = zr = [flipped(k) for k in range(Z)]
    ydev, cdev = dev(z, 1 - y, c), dev(z, y, 1 - c)
    own = (c * 2 + y) * Z
    own_y = (c * 2 + 1 - y) * Z
    slot = own + z

    loads = [pltpu.make_async_copy(fc1_hbm, fc1, wsem.at[0]),
             pltpu.make_async_copy(fc2_hbm, fc2, wsem.at[1])]
    for r in range(SHUF):
        loads.append(pltpu.make_async_copy(
            proj_hbm.at[pl.ds(r * DV, DV)], proj.at[pl.ds(r * DV, DV)], wsem.at[2 + r]))
    loads.append(pltpu.make_async_copy(qkv_hbm, qkv, wsem.at[2 + SHUF]))
    for load in loads:
        load.start()

    barrier = pltpu.get_barrier_semaphore()
    partners = [dev(zs[k], y, c) for k in range(1, Z)] + [ydev, cdev]
    for partner in partners:
        pl.semaphore_signal(barrier, inc=1, device_id=partner, device_id_type=pl.DeviceIdType.MESH)
    pl.semaphore_wait(barrier, len(partners))

    def remote(src, dst, ss, rs, to):
        return pltpu.make_async_remote_copy(
            src_ref=src, dst_ref=dst, send_sem=ss, recv_sem=rs,
            device_id=to, device_id_type=pl.DeviceIdType.MESH)

    def gather(buf, which):
        ss, rs = ag_send.at[which], ag_recv.at[which]
        sent = []

        def send(at, sem, to):
            copy = remote(buf.at[at], buf.at[at], ss.at[sem], rs.at[sem], to)
            copy.start()
            sent.append(copy)

        def arrived(at, sem):
            remote(buf.at[at], buf.at[at], ss.at[sem], rs.at[sem], cdev).wait_recv()

        for k in range(1, Z):
            send(slot, k, dev(zs[k], y, c))
        send(slot, Z, ydev)
        send(slot, 2 * Z, cdev)
        for k in range(1, Z):
            arrived(own + zr[k], k)
            send(own + zr[k], Z + k, ydev)
            send(own + zr[k], 2 * Z + k, cdev)
        for k in range(Z):
            arrived(own_y + zr[k], Z + k)
            send(own_y + zr[k], 3 * Z + k, cdev)
        other = ((1 - c) * 2 + y) * Z
        other_y = ((1 - c) * 2 + 1 - y) * Z
        for k in range(Z):
            arrived(other + zr[k], 2 * Z + k)
        for k in range(Z):
            arrived(other_y + zr[k], 3 * Z + k)
        return sent

    def reduce(buf, ra, ab, rb, ac, rc, which, narrow):
        ss, rs = rs_send.at[which], rs_recv.at[which]
        sent = []

        def send(src, dst, sem, to):
            copy = remote(src, dst, ss.at[sem], rs.at[sem], to)
            copy.start()
            sent.append(copy)

        def arrived(dst, sem):
            remote(dst, dst, ss.at[sem], rs.at[sem], cdev).wait_recv()

        for half in range(2):
            yy = (1 - y) if half == 0 else y
            send(buf.at[pl.ds(((1 - c) * 2 + yy) * Z, Z)], ra.at[half], half, cdev)
        arrived(ra.at[0], 0)
        order = list(range(1, Z)) + [0]
        for k in order:
            narrow(ab.at[k], buf[own_y + zs[k]].astype(F32) + ra[0, zs[k]].astype(F32))
            send(ab.at[k], rb.at[k], 2 + k, ydev)
        arrived(ra.at[1], 1)
        total = None
        for k in order:
            arrived(rb.at[k], 2 + k)
            mine = (buf[own + zs[k]].astype(F32) + ra[1, zs[k]].astype(F32)) + rb[k].astype(F32)
            if k == 0:
                total = mine
            else:
                narrow(ac.at[k], mine)
                send(ac.at[k], rc.at[k], Z + 2 + k, dev(zs[k], y, c))
        for k in range(1, Z):
            arrived(rc.at[k], Z + 2 + k)
            total = total + rc[k].astype(F32)
        return total, sent

    def unpack(buf, width, place=lambda i: i):
        for i in range(n):
            v = buf[i].astype(F32)
            for j in range(width // 128):
                work[j, pl.ds(4 * place(i), 4), :] = v[:, j * 128:(j + 1) * 128]

    def pack(buf, width):
        for i in range(n):
            for j in range(width // 128):
                buf[i, :, pl.ds(j * 128, 128)] = work[j, pl.ds(4 * i, 4), :].astype(BF16)

    values = patches[...].astype(F32)
    mean_sq = jnp.mean(values * values, axis=-1, keepdims=True)
    g1[slot, :, pl.ds(DV, EXT)] = jnp.zeros((SHUF, EXT), BF16)
    g1[slot, :, pl.ds(DV, doc.shape[1])] = jnp.broadcast_to(
        doc[...].astype(F32), (SHUF, doc.shape[1])).astype(BF16)
    normed = values * lax.rsqrt(mean_sq + 1e-6)
    for j in range(DV // 128):
        g1[slot, :, pl.ds(j * 128, 128)] = (
            normed[:, j * 128:(j + 1) * 128] * vit_gain[j:j + 1, :]).astype(BF16)
    sends = gather(g1, 0)

    unpack(g1, DV + EXT)
    lane = lax.broadcasted_iota(jnp.int32, (1, 128), 1)
    for m in range(n // 2):
        low, high = [
            work[DV // 128, pl.ds(4 * (((i % 2) * 2 + (i // 2) % 2) * Z + i // 4), 1), :]
            for i in (2 * m, 2 * m + 1)]
        doc_out[:, pl.ds(m * 128, 128)] = jnp.where(lane < 64, low, pltpu.roll(high, 64, 1))
    for j in range(DV // 128):
        lhs[:, pl.ds(j * 128, 128)] = work[j].astype(BF16)
    loads[0].wait()
    hid_acc[...] = jnp.zeros_like(hid_acc)

    @pl.loop(0, DV // 640)
    def _(j):
        at = pl.ds(pl.multiple_of(j * 640, 128), 640)
        hid_acc[...] += lax.dot_general(
            lhs[:, at], fc1[:, at], (((1,), (1,)), ((), ())), preferred_element_type=F32)

    hidden[...] = gelu(hid_acc[...]).astype(BF16)
    loads[1].wait()

    @pl.loop(0, DV // 640)
    def _(j):
        at = pl.ds(pl.multiple_of(j * 640, 128), 640)
        part = jnp.dot(hidden[...], fc2[:, at], preferred_element_type=F32)
        for m in range(5):
            work[j * 5 + m] = part[:, m * 128:(m + 1) * 128]

    pack(b1, DV)
    total, more = reduce(b1, r1a, a1b, r1b, a1c, r1c, 0, narrow_plain)
    sends += more
    shuffled = (patches[...].astype(F32) + total).astype(BF16).astype(F32)
    row_mean = jnp.sum(jnp.sum(shuffled, axis=1, keepdims=True), axis=0, keepdims=True) / (SHUF * DV)
    centre = shuffled - row_mean
    var = jnp.sum(jnp.sum(centre * centre, axis=1, keepdims=True), axis=0, keepdims=True) / (SHUF * DV)
    normed = centre * lax.rsqrt(var + 1e-5)
    for j in range(DV // 128):
        at = pl.ds(j, SHUF, stride=DV // 128)
        g2[slot, :, pl.ds(j * 128, 128)] = (
            normed[:, j * 128:(j + 1) * 128] * proj_gain[at, :] + proj_bias[at, :]).astype(BF16)
    sends += gather(g2, 1)

    unpack(g2, DV)
    proj_acc[...] = jnp.zeros_like(proj_acc)
    for r in range(SHUF):
        loads[2 + r].wait()
        lhs[:n, :] = jnp.concatenate(
            [work[j, pl.ds(r, n, stride=4), :] for j in range(DV // 128)], axis=1
        ).astype(BF16)

        @pl.loop(0, DV // 640)
        def _(j):
            at = pl.ds(pl.multiple_of(j * 640, 128), 640)
            rows = pl.ds(pl.multiple_of(r * DV + j * 640, 128), 640)
            proj_acc[...] += jnp.dot(lhs[:n, at], proj[rows, :], preferred_element_type=F32)

    projected = gelu(proj_acc[...]).astype(BF16).astype(F32)
    squares = two_parts(jnp.sum(projected * projected, axis=1, keepdims=True))
    scaled = (projected * llm_gain[...]).astype(BF16)
    loads[2 + SHUF].wait()
    for r in range(SHUF):
        for j in range(ROWW // 640):
            part = jnp.dot(scaled, qkv[:, pl.ds(r * ROWW + j * 640, 640)], preferred_element_type=F32)
            for m in range(5):
                work[j * 5 + m, pl.ds(r, n, stride=4), :] = part[:, m * 128:(m + 1) * 128]
        work[ROWW // 128, pl.ds(r, n, stride=4), :] = squares
    pack(b2, ROWW + EXT)
    total, more = reduce(b2, r2a, a2b, r2b, a2c, r2c, 1, narrow_ext)
    sends += more
    square_sum = jnp.sum(total[:, ROWW:], axis=1, keepdims=True)
    inv_rms = lax.rsqrt(square_sum / D + 1e-6)
    cosine, sine = cosine[...], sine[...]
    row = lax.broadcasted_iota(jnp.int32, (SHUF, HD), 0)
    for h in range(ROWW // HD):
        x = total[:, h * HD:(h + 1) * HD] * inv_rms
        turned = x * cosine + pltpu.roll(x, HD // 2, 1) * sine
        g3[slot, :, pl.ds(h * HD, HD)] = jnp.where(
            row * (ROWW // HD) + h < QH + KVH, turned, x).astype(BF16)
    sends += gather(g3, 2)
    unpack(g3, ROWW, lambda i: (i % Z) * 4 + (i // Z) % 2 * 2 + i // (2 * Z))
    for r in range(SHUF):
        for j in range(ROWW // HD):
            out[:, pl.ds(r * ROWW + j * HD, HD)] = work[j, pl.ds(r, n, stride=4), :].astype(BF16)
    for copy in sends:
        copy.wait_send()


def image_rows(n, patches, vit_gain, fc1, fc2, proj_gain, proj_bias, proj, llm_gain, qkv, cosine, sine, doc):
    Z = n // 4
    vm = pl.BlockSpec(memory_space=pltpu.VMEM)
    hbm = pl.BlockSpec(memory_space=pl.ANY)

    def reduce_bufs(width):
        return [
            pltpu.VMEM((n, SHUF, width), BF16),
            pltpu.VMEM((2, Z, SHUF, width), BF16),
        ] + [pltpu.VMEM((Z, SHUF, width), BF16)] * 4

    hid = fc1.shape[0]
    cols = proj.shape[1]
    weights = sum(w.size for w in (fc1, fc2, proj, qkv))
    return pl.pallas_call(
        functools.partial(image_kernel, n),
        out_shape=(
            jax.ShapeDtypeStruct((n, SHUF * ROWW), BF16),
            jax.ShapeDtypeStruct((1, n * HD // 2), F32),
        ),
        in_specs=[vm, vm, hbm, hbm, vm, vm, hbm, vm, hbm, vm, vm, vm],
        out_specs=(vm, vm),
        scratch_shapes=[
            pltpu.VMEM(fc1.shape, BF16),
            pltpu.VMEM(fc2.shape, BF16),
            pltpu.VMEM(proj.shape, BF16),
            pltpu.VMEM(qkv.shape, BF16),
            pltpu.VMEM((n, SHUF, DV + EXT), BF16),
            pltpu.VMEM((n, SHUF, DV), BF16),
            pltpu.VMEM((n, SHUF, ROWW), BF16),
        ] + reduce_bufs(DV) + reduce_bufs(ROWW + EXT) + [
            pltpu.VMEM((DV // 128 + 1, n * SHUF, 128), F32),
            pltpu.VMEM((n * SHUF, DV), BF16),
            pltpu.VMEM((n * SHUF, hid), F32),
            pltpu.VMEM((n * SHUF, hid), BF16),
            pltpu.VMEM((n, cols), F32),
            pltpu.SemaphoreType.DMA((3 + SHUF,)),
            pltpu.SemaphoreType.DMA((3, 4 * Z)),
            pltpu.SemaphoreType.DMA((3, 4 * Z)),
            pltpu.SemaphoreType.DMA((2, 2 * Z + 2)),
            pltpu.SemaphoreType.DMA((2, 2 * Z + 2)),
        ],
        compiler_params=pltpu.CompilerParams(
            collective_id=0, has_side_effects=True, vmem_limit_bytes=56 * 2 ** 20),
        cost_estimate=pl.CostEstimate(
            flops=64 * weights, bytes_accessed=2 * weights, transcendentals=0),
    )(patches, vit_gain, fc1, fc2, proj_gain, proj_bias, proj, llm_gain, qkv, cosine, sine, doc)


def attend_kernel(n, span, width, query, keys, vals, doc, pos, iq, ik, iv, out, bias, hit_k, img_k, hit_q, img_q):
    rows = query.shape[0]
    me = lax.axis_index("ctx")
    first = jnp.clip(lax.div(jnp.maximum(me - span, 0), 2) * 2, 0, n - width // rows) * rows
    first = pl.multiple_of(first, 2 * rows)
    group = QH // KVH

    @pl.when(pl.program_id(0) == 0)
    def _():
        docs = doc[...]
        q_pos = me * rows + lax.broadcasted_iota(jnp.int32, (rows, docs.shape[1]), 0)
        k_pos = lax.broadcasted_iota(jnp.int32, (rows, docs.shape[1]), 1)
        q_doc = jnp.sum(jnp.where(q_pos == k_pos, docs, 0.0), axis=1, keepdims=True)
        k_doc = doc[:, pl.ds(first, width)]
        ok = (first + k_pos[:, :width] <= q_pos[:, :width]) & (k_doc == q_doc)
        bias[...] = jnp.where(ok, 0.0, -1e30)

        def hits(count, start):
            at = start + lax.broadcasted_iota(jnp.int32, (count, n), 0)
            hit = (at == pos[...]).astype(F32)
            return hit.astype(BF16), jnp.sum(hit, axis=1, keepdims=True)

        table, live = hits(width, first)
        hit_k[...] = table
        img_k[...] = jnp.broadcast_to(live, img_k.shape)
        table, live = hits(rows, me * rows)
        hit_q[...] = table
        img_q[...] = jnp.broadcast_to(live, img_q.shape)

    def put(live, table, image, text):
        placed = jnp.dot(table, image, preferred_element_type=F32)
        return jnp.where(live > 0.0, placed, text.astype(F32)).astype(BF16)

    k = put(img_k[...], hit_k[...], ik[...], keys[pl.ds(first, width), :])
    v = put(img_k[...], hit_k[...], iv[...], vals[pl.ds(first, width), :])
    scale = HD ** -0.5 * 1.4426950408889634
    table = jnp.concatenate([bias[...]] * 4, axis=0)
    for m in range(0, group, 4):
        heads = [slice((m + i) * HD, (m + i + 1) * HD) for i in range(4)]
        q = jnp.concatenate(
            [put(img_q[...], hit_q[...], iq[:, at], query[:, at]) for at in heads], axis=0)
        s = lax.dot_general(q, k, (((1,), (1,)), ((), ())), preferred_element_type=F32)
        s = s + table
        w = jnp.exp2((s - jnp.max(s, axis=1, keepdims=True)) * scale)
        total = jnp.sum(w, axis=1, keepdims=True)
        o = (jnp.dot(w.astype(BF16), v, preferred_element_type=F32) / total).astype(BF16)
        for i in range(4):
            out[:, heads[i]] = o[i * rows:(i + 1) * rows]


def attention(n, query, keyvalue, doc, pos, image):
    rows = query.shape[0]
    seq = keyvalue.shape[0]
    group = QH // KVH
    span = seq * 5 // 8 // rows
    width = min(span + 2, n) * rows
    return pl.pallas_call(
        functools.partial(attend_kernel, n, span, width),
        grid=(KVH,),
        out_shape=jax.ShapeDtypeStruct((rows, QH * HD), BF16),
        in_specs=[
            pl.BlockSpec((rows, group * HD), lambda g: (0, g)),
            pl.BlockSpec((seq, HD), lambda g: (0, g)),
            pl.BlockSpec((seq, HD), lambda g: (0, KVH + g)),
            pl.BlockSpec((1, seq), lambda g: (0, 0)),
            pl.BlockSpec((1, n), lambda g: (0, 0)),
            pl.BlockSpec((n, group * HD), lambda g: (0, g)),
            pl.BlockSpec((n, HD), lambda g: (0, QH + g)),
            pl.BlockSpec((n, HD), lambda g: (0, QH + KVH + g)),
        ],
        out_specs=pl.BlockSpec((rows, group * HD), lambda g: (0, g)),
        scratch_shapes=[
            pltpu.VMEM((rows, width), F32),
            pltpu.VMEM((width, n), BF16),
            pltpu.VMEM((width, HD), F32),
            pltpu.VMEM((rows, n), BF16),
            pltpu.VMEM((rows, HD), F32),
        ],
        compiler_params=pltpu.CompilerParams(vmem_limit_bytes=60 * 2 ** 20),
        cost_estimate=pl.CostEstimate(
            flops=4 * rows * QH * HD * width, bytes_accessed=4 * query.size + 2 * keyvalue.size,
            transcendentals=rows * QH * width),
    )(query, keyvalue, keyvalue, doc, pos, image, image, image)


def shards(
    n,
    patches,
    vit_gain,
    vit_fc1,
    vit_fc2,
    proj_gain,
    proj_bias,
    proj_weight,
    llm_gain,
    qkv_weight,
    text_query,
    text_keyvalue,
    doc_ids,
    image_positions,
):
    kv_all = lax.all_gather(text_keyvalue, "ctx", axis=0, tiled=True)
    doc = doc_ids.reshape(1, -1)
    half = HD // 2
    lane = lax.broadcasted_iota(jnp.int32, (1, HD), 1)
    inv_freq = 1000000.0 ** (-2.0 * (lane % half).astype(F32) / HD)
    own_pos = lax.dynamic_index_in_dim(image_positions, lax.axis_index("ctx"), 0, keepdims=False)
    angle = own_pos.astype(F32) * inv_freq
    cosine, sine = jnp.cos(angle), jnp.where(lane < half, -jnp.sin(angle), jnp.sin(angle))
    image, doc_all = image_rows(
        n, patches, vit_gain.reshape(-1, 128), vit_fc1.T, vit_fc2,
        proj_gain.reshape(-1, 128), proj_bias.reshape(-1, 128), proj_weight,
        llm_gain.reshape(1, -1), qkv_weight, cosine, sine, doc)
    return attention(
        n, text_query, kv_all, doc_all, image_positions.reshape(1, -1), image)


def solution(mesh):
    placed = (
        P(("groups", "ctx"), None),
        P(),
        P(None, "ctx"),
        P("ctx", None),
        P(),
        P(),
        P(None, "ctx"),
        P("ctx"),
        P("ctx", None),
        P(("groups", "ctx"), None),
        P(("groups", "ctx"), None),
        P(("groups", "ctx")),
        P("groups"),
    )
    return jax.shard_map(
        functools.partial(shards, mesh.shape["ctx"]), mesh=mesh, in_specs=placed,
        out_specs=P(("groups", "ctx"), None), check_vma=False)
```
